32 devices in a mesh: groups: 2 (over y), seq: 4 (over z), head: 2 (over x), batch: 2 (over core).
Axes of the slice: x: 2, y: 2, z: 4, core: 2. Of those that a mesh axis runs over, the one named last changes fastest.
Arguments:
- query_rows: bfloat16 [4, 4096, 1024], P(('groups', 'batch'), 'seq', 'head'), parts along dimension 0, may hold values from -32 to 32
- key_rows: bfloat16 [4, 4096, 1024], P(('groups', 'batch'), 'seq', 'head'), parts along dimension 0, may hold values from -32 to 32
- value_rows: bfloat16 [4, 4096, 1024], P(('groups', 'batch'), 'seq', 'head'), parts along dimension 0, may hold values from -6 to 6
- grad_output: bfloat16 [4, 4096, 1024], P(('groups', 'batch'), 'seq', 'head'), parts along dimension 0, may hold values from -6 to 6
Outputs:
- grad_queries: bfloat16 [4, 4096, 1024], P(('groups', 'batch'), 'seq', 'head'), parts along dimension 0
- grad_keys: bfloat16 [4, 4096, 1024], P(('groups', 'batch'), 'seq', 'head'), parts along dimension 0
- grad_values: bfloat16 [4, 4096, 1024], P(('groups', 'batch'), 'seq', 'head'), parts along dimension 0
The draws below stay inside these ranges and needn't reach their ends.
There are 2 independent parts, one for each index of `groups`. The reference program is written for one: setup_inputs(seed, part) draws one part's arguments, and reference() takes and returns one part's arrays. A program takes and returns all parts, laid end to end along the dimension named above; each array names one. Nothing has to cross between parts.
All inputs are finite; a program needn't handle non-finite values. Where the reference program divides by a largest or mean magnitude, that divisor is 1e-20 or more.
Results may differ from the reference program's by a relative error of at most 0.023.
The reference program's roundings to bfloat16 on the way (of `land_q`, `land_k`, `weights_b`, `combined`, `dsf` and `dsb`) count: a program that leaves them out, or rounds other values in their place, can miss the bound.
Values may be sent and summed in bfloat16 or wider, within the bound.
A program may use at most 128 MiB of HBM per device.

```python
import jax
import jax.numpy as jnp
from jax import lax

DH = 64
HEADS = 16
M = 256
ITERS = 4
WIDTH = 1024
LEN = 4096
SEQS = 2
SEG = 16


def shared_centers(key, scale):
    return scale * jax.random.normal(jax.random.fold_in(key, 7), (SEQS, M, WIDTH), jnp.float32)


def segment_draw(key, salt):
    centers = shared_centers(key, 0.8)
    noise = 0.6 * jax.random.normal(jax.random.fold_in(key, salt + 1), (SEQS, LEN, WIDTH), jnp.float32)
    return jnp.clip(jnp.repeat(centers, SEG, axis=1) + noise, -32.0, 32.0)


def draw_query_rows(key, part):
    return segment_draw(key, 11).astype(jnp.bfloat16)


def draw_key_rows(key, part):
    return segment_draw(key, 23).astype(jnp.bfloat16)


def shard_levels(own_key, shape, cuts, least, largest):
    level, own = 1.0, jax.random.fold_in(own_key, 6)
    for dim, shards_of in cuts:
        heights = jnp.exp(jax.random.uniform(jax.random.fold_in(own, dim), (shards_of,), jnp.float32, least / len(cuts), largest / len(cuts)))
        level = level * jnp.repeat(heights, shape[dim] // shards_of).reshape([-1 if axis == dim else 1 for axis in range(len(shape))])
    return level


def gaussian(own_key, extent, scale, bound, shards=(), kind=jnp.bfloat16):
    entries = scale * jax.random.normal(own_key, extent, jnp.float32)
    if shards:
        entries = entries * shard_levels(own_key, extent, shards, -0.22, 0.18)
    return jnp.clip(entries, -bound, bound).astype(kind)


def setup_inputs(seed: int = 0, part: int = 0) -> dict:
    key_list = jax.random.split(jax.random.key(seed), 5)
    own_keys = jax.random.split(jax.random.fold_in(key_list[4], part), 5)
    return {
        "query_rows": draw_query_rows(jax.random.fold_in(jax.random.fold_in(key_list[4], part), 71), part),
        "key_rows": draw_key_rows(jax.random.fold_in(jax.random.fold_in(key_list[4], part), 71), part),
        "value_rows": gaussian(own_keys[2], (SEQS, LEN, WIDTH), 1.0, 6.0, ((0, 2), (1, 4), (2, 2))),
        "grad_output": gaussian(own_keys[3], (SEQS, LEN, WIDTH), 1.0, 6.0, ((0, 2), (1, 4), (2, 2))),
    }


def newton(matrix):
    size = matrix.shape[-1]
    identity = jnp.eye(size, dtype=matrix.dtype)
    col_norm = lax.optimization_barrier(jnp.max(lax.optimization_barrier(jnp.sum(jnp.abs(matrix), axis=-2)), axis=-1))
    row_norm = lax.optimization_barrier(jnp.max(lax.optimization_barrier(jnp.sum(jnp.abs(matrix), axis=-1)), axis=-1))
    approx = jnp.swapaxes(matrix, -1, -2) / (col_norm * row_norm)[..., None, None]
    for sweep in range(ITERS):
        product = jnp.matmul(matrix, approx, precision=lax.Precision.HIGHEST)
        inner = jnp.matmul(product, 7.0 * identity - product, precision=lax.Precision.HIGHEST)
        inner = jnp.matmul(product, 15.0 * identity - inner, precision=lax.Precision.HIGHEST)
        approx = 0.25 * jnp.matmul(approx, 13.0 * identity - inner, precision=lax.Precision.HIGHEST)
    return approx

def normalize(scores):
    shifted = jnp.exp(scores - lax.optimization_barrier(jnp.max(scores, axis=-1, keepdims=True)))
    return shifted / lax.optimization_barrier(jnp.sum(shifted, axis=-1, keepdims=True))

def one_head(query, keyrow, value, grad):
    high = lax.Precision.HIGHEST
    temper = DH ** (-0.5)
    land_q = (lax.optimization_barrier(jnp.sum(query.reshape(M, SEG, DH), axis=1, dtype=jnp.float32)) / SEG).astype(jnp.bfloat16)
    land_k = (lax.optimization_barrier(jnp.sum(keyrow.reshape(M, SEG, DH), axis=1, dtype=jnp.float32)) / SEG).astype(jnp.bfloat16)
    soft_f = normalize(temper * jnp.dot(query, land_k.T, preferred_element_type=jnp.float32))
    soft_a = normalize(temper * jnp.dot(land_q, land_k.T, preferred_element_type=jnp.float32))
    inverse, pull = jax.vjp(newton, soft_a)
    soft_b = normalize(temper * jnp.dot(land_q, keyrow.T, preferred_element_type=jnp.float32))
    weights_b = soft_b.astype(jnp.bfloat16)
    mixed = jnp.dot(weights_b, value, preferred_element_type=jnp.float32)
    combined = jnp.dot(inverse, mixed, precision=high).astype(jnp.bfloat16)
    weights_f = soft_f.astype(jnp.bfloat16)
    grad_comb = jnp.dot(weights_f.T, grad, preferred_element_type=jnp.float32)
    grad_f = jnp.dot(grad, combined.T, preferred_element_type=jnp.float32)
    dsf = (soft_f * (grad_f - lax.optimization_barrier(jnp.sum(grad_f * soft_f, axis=-1, keepdims=True)))).astype(jnp.bfloat16)
    dq_local = temper * jnp.dot(dsf, land_k, preferred_element_type=jnp.float32)
    key_land_f = temper * jnp.dot(dsf.T, query, preferred_element_type=jnp.float32)
    grad_inv = jnp.dot(grad_comb, mixed.T, precision=high)
    grad_mix = jnp.dot(inverse.T, grad_comb, precision=high)
    grad_a = pull(grad_inv)[0]
    dsa = soft_a * (grad_a - lax.optimization_barrier(jnp.sum(grad_a * soft_a, axis=-1, keepdims=True)))
    query_land_a = temper * jnp.dot(dsa, land_k.astype(jnp.float32), precision=high)
    key_land_a = temper * jnp.dot(dsa.T, land_q.astype(jnp.float32), precision=high)
    gmix = grad_mix.astype(jnp.bfloat16)
    grad_b = jnp.dot(gmix, value.T, preferred_element_type=jnp.float32)
    row_dot = lax.optimization_barrier(jnp.sum(gmix.astype(jnp.float32) * mixed, axis=-1, keepdims=True))
    dsb = (soft_b * (grad_b - row_dot)).astype(jnp.bfloat16)
    grad_vals = jnp.dot(weights_b.T, gmix, preferred_element_type=jnp.float32).astype(jnp.bfloat16)
    query_land_b = temper * jnp.dot(dsb, keyrow, preferred_element_type=jnp.float32)
    dk_local = temper * jnp.dot(dsb.T, land_q, preferred_element_type=jnp.float32)
    query_land = (query_land_b + query_land_a) / SEG
    key_land = (key_land_f + key_land_a) / SEG
    grad_q = (dq_local.reshape(M, SEG, DH) + query_land[:, None, :]).reshape(LEN, DH)
    grad_k = (dk_local.reshape(M, SEG, DH) + key_land[:, None, :]).reshape(LEN, DH)
    return (grad_q.astype(jnp.bfloat16), grad_k.astype(jnp.bfloat16), grad_vals)

def split_heads(data):
    return data.reshape(SEQS, LEN, HEADS, DH).transpose(0, 2, 1, 3).reshape(SEQS * HEADS, LEN, DH)

def join_heads(data):
    return data.reshape(SEQS, HEADS, LEN, DH).transpose(0, 2, 1, 3).reshape(SEQS, LEN, WIDTH)

def reference(query_rows, key_rows, value_rows, grad_output):
    stacked = (split_heads(query_rows), split_heads(key_rows), split_heads(value_rows), split_heads(grad_output))
    grad_q, grad_k, grad_v = lax.map(lambda items: one_head(items[0], items[1], items[2], items[3]), stacked)
    return (join_heads(grad_q), join_heads(grad_k), join_heads(grad_v))
```

```python
import functools
import math

import jax
import jax.numpy as jnp
from jax import lax
from jax.experimental import pallas as pl
from jax.experimental.pallas import tpu as pltpu
from jax.sharding import PartitionSpec as P

DH = 64
M = 256
ITERS = 4
PAIR = 2 * DH
TEMPER = DH ** (-0.5)
LOG2 = TEMPER * math.log2(math.e)
F32, BF16 = jnp.float32, jnp.bfloat16
HIGH = lax.Precision.HIGH
VMEM_LIMIT = 56 * 1024 * 1024


def mm(a, b, prec=None):
    return lax.dot_general(a, b, (((1,), (0,)), ((), ())), precision=prec, preferred_element_type=F32)


def nt(a, b, prec=None):
    return lax.dot_general(a, b, (((1,), (1,)), ((), ())), precision=prec, preferred_element_type=F32)


def tn(a, b, prec=None):
    return lax.dot_general(a, b, (((0,), (0,)), ((), ())), precision=prec, preferred_element_type=F32)


def own_half(shape, head):
    lane = lax.broadcasted_iota(jnp.int32, shape, len(shape) - 1)
    return lane < DH if head == 0 else lane >= DH


def only(x, head):
    return jnp.where(own_half(x.shape, head), x, jnp.zeros_like(x))


def stacked(x):
    return jnp.concatenate([only(x, 0), only(x, 1)], axis=0)


def halves(x):
    return jnp.where(own_half((M, PAIR), 0), x[:M], x[M:])


def landmark_kernel(q_ref, k_ref, out_ref):
    rows = q_ref.shape[0]
    land = out_ref.shape[1]
    seg = rows // land
    spot = lax.broadcasted_iota(jnp.int32, (land, rows), 0)
    place = lax.broadcasted_iota(jnp.int32, (land, rows), 1)
    member = jnp.where((place >= spot * seg) & (place < spot * seg + seg), 1.0, 0.0).astype(BF16)
    out_ref[0] = (mm(member, q_ref[...]) / seg).astype(BF16)
    out_ref[1] = (mm(member, k_ref[...]) / seg).astype(BF16)


def first_kernel(q_ref, k_ref, v_ref, g_ref, land_ref, wf_ref, eb_ref, mix_ref, comb_ref, stat_ref):
    lq, lk = stacked(land_ref[0]), stacked(land_ref[1])
    rows = q_ref.shape[0]
    for h in range(2):
        sf = nt(lk[h * M : (h + 1) * M], q_ref[...])
        top = jnp.max(sf, axis=0, keepdims=True)
        ef = jnp.exp2((sf - top) * LOG2)
        wf_ref[0, h * M : (h + 1) * M] = (ef * (1.0 / jnp.sum(ef, axis=0, keepdims=True))).astype(BF16)
    comb_ref[0] = halves(mm(wf_ref[0], g_ref[...]))
    tops, mixes = [], []
    for h in range(2):
        sb = nt(lq[h * M : (h + 1) * M], k_ref[...])
        top = jnp.max(sb, axis=1, keepdims=True)
        eb = jnp.exp2((sb - top) * LOG2).astype(BF16)
        eb_ref[0, h * M : (h + 1) * M] = eb
        values = jnp.where(own_half((rows, PAIR), h), v_ref[...], jnp.ones_like(v_ref[...]))
        mixes.append(mm(eb, values))
        tops.append(jnp.broadcast_to(top, (M, PAIR)))
    low = own_half((M, PAIR), 0)
    mix_ref[0] = jnp.where(low, mixes[0], mixes[1])
    total = jnp.where(low, mixes[1], mixes[0])
    tall = jnp.where(low, tops[1], tops[0])
    tall_t, total_t = tall.T, total.T
    stat_ref[0] = jnp.concatenate(
        [tall_t[DH : DH + 1], tall_t[0:1], total_t[DH : DH + 1], total_t[0:1], jnp.zeros((4, M), F32)], axis=0
    )


def forward_kernel(land_ref, soft_ref, x_ref, y_ref, q_ref, inv_ref):
    lq, lk = land_ref[0], land_ref[1]
    rowi = lax.broadcasted_iota(jnp.int32, (M, M), 0)
    coli = lax.broadcasted_iota(jnp.int32, (M, M), 1)
    eye = jnp.where(rowi == coli, 1.0, 0.0)
    soft, scale, xs, prods = [], [], [], []
    for h in range(2):
        s = nt(only(lq, h), lk)
        e = jnp.exp2((s - jnp.max(s, axis=1, keepdims=True)) * LOG2)
        a = e / jnp.sum(e, axis=1, keepdims=True)
        soft_ref[0, h] = a
        inv_s = 1.0 / (jnp.max(jnp.sum(a, axis=0, keepdims=True), axis=1, keepdims=True)
                       * jnp.max(jnp.sum(a, axis=1, keepdims=True), axis=0, keepdims=True))
        soft.append(a)
        scale.append(inv_s)
        xs.append(nt(a, a, HIGH) * inv_s)
        prods.append(None)
    for k in range(ITERS):
        ys = [mm(x, x, HIGH) for x in xs]
        ts = [mm(x, y, HIGH) for x, y in zip(xs, ys)]
        for h in range(2):
            x_ref[0, h, k] = xs[h]
            y_ref[0, h, k] = ys[h]
            q = 3.25 * eye - 3.75 * xs[h] + 1.75 * ys[h] - 0.25 * ts[h]
            q_ref[0, h, k] = q
            prods[h] = q if k == 0 else mm(prods[h], q, HIGH)
            if k < ITERS - 1:
                xs[h] = mm(xs[h], q, HIGH)
    for h in range(2):
        inv_ref[0, h] = tn(soft[h], prods[h], HIGH) * scale[h]


def middle_kernel(parts, dests, mine, mix_ref, comb_ref, stat_ref, inv_ref, full_ref, send_ref):
    low = own_half((M, PAIR), 0)
    stats = []
    for d in range(parts):
        st = stat_ref[d, 0]
        def column(r0, r1):
            wide = jnp.concatenate([jnp.broadcast_to(st[r0 : r0 + 1], (DH, M)), jnp.broadcast_to(st[r1 : r1 + 1], (DH, M))], axis=0)
            return wide.T
        stats.append((column(0, 1), column(2, 3)))
    top = functools.reduce(jnp.maximum, [s[0] for s in stats])
    shrink = [jnp.exp2((s[0] - top) * LOG2) for s in stats]
    total = sum(f * s[1] for f, s in zip(shrink, stats))
    inv_total = 1.0 / total
    mixed = sum(f * mix_ref[d, 0].astype(F32) for d, f in enumerate(shrink)) * inv_total
    gcomb = sum(comb_ref[d, 0].astype(F32) for d in range(parts))
    full_ref[0, 0] = mixed
    full_ref[0, 1] = gcomb
    comb, gm = [], []
    for h in range(2):
        comb.append(mm(inv_ref[0, h], only(mixed, h), HIGH))
        gm.append(tn(inv_ref[0, h], only(gcomb, h), HIGH))
    combined = comb[0] + comb[1]
    gmix = gm[0] + gm[1]
    full_ref[0, 2] = combined
    for i in range(dests):
        if dests == parts:
            factor = shrink[i] * inv_total
        else:
            me = lax.axis_index("seq")
            own = sum(jnp.where(me == d, shrink[d], 0.0) for d in range(parts))
            factor = own * inv_total
        scaled = (gmix * factor).astype(BF16)
        send_ref[i, 0, 0:M] = combined.astype(BF16)
        dot = scaled.astype(F32) * mixed
        for h in range(2):
            rd = -jnp.sum(only(dot, h), axis=1, keepdims=True)
            hi = rd.astype(BF16)
            lo = (rd - hi.astype(F32)).astype(BF16)
            lane = lax.broadcasted_iota(jnp.int32, (M, PAIR), 1)
            start = DH if h == 0 else 0
            zero = jnp.zeros((M, PAIR), BF16)
            rest = jnp.where(lane == start, jnp.broadcast_to(hi, (M, PAIR)), jnp.where(lane == start + 1, jnp.broadcast_to(lo, (M, PAIR)), zero))
            send_ref[i, 0, (1 + h) * M : (2 + h) * M] = jnp.where(own_half((M, PAIR), h), scaled, rest)


def sym(x):
    return 0.5 * (x + x.T)


def backward_kernel(land_ref, soft_ref, x_ref, y_ref, q_ref, full_ref, out_ref):
    mixed, gcomb, combined = full_ref[0, 0], full_ref[0, 1], full_ref[0, 2]
    soft = [soft_ref[0, h] for h in range(2)]
    col = [jnp.sum(a, axis=0, keepdims=True) for a in soft]
    row = [jnp.sum(a, axis=1, keepdims=True) for a in soft]
    cn = [jnp.max(c, axis=1, keepdims=True) for c in col]
    rn = [jnp.max(r, axis=0, keepdims=True) for r in row]
    inv_s = [1.0 / (c * r) for c, r in zip(cn, rn)]
    gc = [only(gcomb, h) for h in range(2)]
    us = [[mm(soft[h], gc[h], HIGH) * inv_s[h]] for h in range(2)]
    ms = [[only(mixed, h)] for h in range(2)]
    for k in range(ITERS - 1):
        for h in range(2):
            us[h].append(mm(q_ref[0, h, k], us[h][-1], HIGH))
            ms[h].append(mm(q_ref[0, h, ITERS - 1 - k], ms[h][-1], HIGH))
    rm = [mm(q_ref[0, h, 0], ms[h][-1], HIGH) for h in range(2)]
    b = [None, None]
    for k in reversed(range(ITERS)):
        xs = [x_ref[0, h, k] for h in range(2)]
        ys = [y_ref[0, h, k] for h in range(2)]
        c = []
        for h in range(2):
            u, m = us[h][k], ms[h][ITERS - 1 - k]
            c.append(0.5 * nt(u + pltpu.roll(m, DH, 1), m + pltpu.roll(u, DH, 1), HIGH))
        t = [-0.25 * c[h] if b[h] is None else 1.75 * b[h] - 0.25 * c[h] for h in range(2)]
        tx = [mm(t[h], xs[h], HIGH) for h in range(2)]
        ty = [mm(t[h], ys[h], HIGH) for h in range(2)]
        for h in range(2):
            if b[h] is None:
                yb = 1.75 * c[h] + sym(tx[h])
                xb = -3.75 * c[h]
            else:
                by = mm(b[h], ys[h], HIGH)
                yb = 1.75 * c[h] - 3.75 * b[h] + sym(tx[h] - 0.5 * by)
                xb = 3.25 * b[h] - 3.75 * c[h]
            b[h] = xb + sym(ty[h] + 2.0 * mm(yb, xs[h], HIGH))
    lq, lk = land_ref[0].astype(F32), land_ref[1].astype(F32)
    qa, ka = [], []
    for h in range(2):
        a = soft[h]
        sbar = -inv_s[h] * (
            jnp.sum(jnp.sum(gc[h] * combined, axis=1, keepdims=True), axis=0, keepdims=True)
            + jnp.sum(jnp.sum(b[h] * x_ref[0, h, 0], axis=1, keepdims=True), axis=0, keepdims=True)
        )
        grad = inv_s[h] * (nt(rm[h], gc[h], HIGH) + 2.0 * mm(b[h], a, HIGH))
        atc = jnp.where(col[h] == cn[h], 1.0, 0.0)
        atr = jnp.where(row[h] == rn[h], 1.0, 0.0)
        grad += atc * (sbar * rn[h] / jnp.sum(atc, axis=1, keepdims=True))
        grad += atr * (sbar * cn[h] / jnp.sum(atr, axis=0, keepdims=True))
        dsa = a * (grad - jnp.sum(grad * a, axis=1, keepdims=True))
        qa.append(mm(dsa, lk, HIGH))
        ka.append(tn(dsa, lq, HIGH))
    low = own_half((M, PAIR), 0)
    out_ref[0, 0] = TEMPER * jnp.where(low, qa[0], qa[1])
    out_ref[0, 1] = TEMPER * jnp.where(low, ka[0], ka[1])


def second_kernel(q_ref, k_ref, v_ref, g_ref, land_ref, wf_ref, eb_ref, got_ref, dq_ref, dk_ref, gv_ref, part_ref):
    lq, lk = stacked(land_ref[0]), stacked(land_ref[1])
    rows = q_ref.shape[0]
    comb = stacked(got_ref[0, 0:M])
    dsf = []
    for h in range(2):
        gf = nt(comb[h * M : (h + 1) * M], g_ref[...])
        w = wf_ref[0, h * M : (h + 1) * M].astype(F32)
        r = jnp.sum(gf * w, axis=0, keepdims=True)
        dsf.append((w * (gf - r)).astype(BF16))
    dsf = jnp.concatenate(dsf, axis=0)
    dq_ref[...] = TEMPER * tn(lk, dsf).T
    part_ref[1] = TEMPER * halves(mm(dsf, q_ref[...]))
    dsb, gms = [], []
    for h in range(2):
        gx = got_ref[0, (1 + h) * M : (2 + h) * M]
        values = jnp.where(own_half((rows, PAIR), h), v_ref[...], jnp.ones_like(v_ref[...]))
        gb = nt(gx, values)
        dsb.append((eb_ref[0, h * M : (h + 1) * M].astype(F32) * gb).astype(BF16))
        gms.append(only(gx, h))
    dsb = jnp.concatenate(dsb, axis=0)
    gms = jnp.concatenate(gms, axis=0)
    gv_ref[...] = tn(gms, eb_ref[0]).T.astype(BF16)
    part_ref[0] = TEMPER * halves(mm(dsb, k_ref[...]))
    dk_ref[...] = TEMPER * tn(lq, dsb).T


def last_kernel(parts, dq_ref, dk_ref, got_ref, gq_ref, gk_ref):
    land = got_ref.shape[2]
    rows = dq_ref.shape[0]
    seg = rows // land
    for i, (src, dst) in enumerate(((dq_ref, gq_ref), (dk_ref, gk_ref))):
        total = sum(got_ref[d, i].astype(F32) for d in range(parts)) / seg
        wide = jnp.broadcast_to(total[:, None, :], (land, seg, PAIR)).reshape(rows, PAIR)
        dst[...] = (src[...] + wide).astype(BF16)


def params():
    return pltpu.CompilerParams(vmem_limit_bytes=VMEM_LIMIT)


def cost(flops, moved):
    return pl.CostEstimate(flops=int(flops), bytes_accessed=int(moved), transcendentals=0)


def shape(dims, dtype=F32):
    return jax.ShapeDtypeStruct(dims, dtype)


def spread_out(x, spread, personal):
    me = lax.axis_index("seq")
    def to(d):
        return lax.dynamic_index_in_dim(x, d, 0, keepdims=False) if personal else x
    got = [to(me)]
    for step in range(1, spread):
        perm = [(i, (i + step) % spread) for i in range(spread)]
        got.append(lax.ppermute(to(lax.rem(me + step, spread)), "seq", perm))
    table = jnp.stack(got)
    return jnp.stack([lax.dynamic_index_in_dim(table, lax.rem(me - s + spread, spread), 0, keepdims=False) for s in range(spread)])


def per_device(query_rows, key_rows, value_rows, grad_output):
    _, rows, width = query_rows.shape
    q, k, v, g = (x[0] for x in (query_rows, key_rows, value_rows, grad_output))
    spread = lax.axis_size("seq")
    me = lax.axis_index("seq")
    land_dev = M // spread
    pairs = width // PAIR
    shared = pairs == spread
    owned = 1 if shared else pairs

    land = pl.pallas_call(landmark_kernel, out_shape=shape((2, land_dev, width), BF16), compiler_params=params())(q, k)
    land = spread_out(land, spread, False)
    land = jnp.swapaxes(land, 0, 1).reshape(2, M, width)

    cols = pl.BlockSpec((rows, PAIR), lambda p: (0, p))
    lands = pl.BlockSpec((2, M, PAIR), lambda p: (0, 0, p))
    def lead(*dims):
        return pl.BlockSpec((1,) + dims, lambda p: (p,) + (0,) * len(dims))
    wf, eb, mix, comb, stat = pl.pallas_call(
        first_kernel,
        grid=(pairs,),
        in_specs=[cols] * 4 + [lands],
        out_specs=[lead(2 * M, rows), lead(2 * M, rows), lead(M, PAIR), lead(M, PAIR), lead(8, M)],
        out_shape=[shape((pairs, 2 * M, rows), BF16), shape((pairs, 2 * M, rows), BF16), shape((pairs, M, PAIR)), shape((pairs, M, PAIR)), shape((pairs, 8, M))],
        compiler_params=params(),
    )(q, k, v, g, land)

    land_own = lax.dynamic_slice_in_dim(land, me * PAIR, PAIR, 2) if shared else land
    squares = lead(2, M, M)
    steps = lead(2, ITERS, M, M)
    soft, xs, ys, qs, inv = pl.pallas_call(
        forward_kernel,
        grid=(owned,),
        in_specs=[lands],
        out_specs=[squares, steps, steps, steps, squares],
        out_shape=[shape((owned, 2, M, M))] + [shape((owned, 2, ITERS, M, M))] * 3 + [shape((owned, 2, M, M))],
        compiler_params=params(),
        cost_estimate=cost(16 * 12 * M**3 * 2 * owned, 8 * 2**20 * owned),
    )(land_own)

    if shared:
        bundle = jnp.concatenate([mix, comb], axis=1).astype(BF16)
        bundle = spread_out(bundle, spread, True)
        stat = spread_out(stat, spread, True)
        mix_all, comb_all, stat_all = bundle[:, None, :M], bundle[:, None, M:], stat[:, None]
    else:
        mix_all, comb_all, stat_all = (lax.all_gather(x, "seq") for x in (mix, comb, stat))
    dests = spread if shared else 1
    full, send = pl.pallas_call(
        functools.partial(middle_kernel, spread, dests, None),
        grid=(owned,),
        in_specs=[
            pl.BlockSpec((spread, 1, M, PAIR), lambda p: (0, p, 0, 0)),
            pl.BlockSpec((spread, 1, M, PAIR), lambda p: (0, p, 0, 0)),
            pl.BlockSpec((spread, 1, 8, M), lambda p: (0, p, 0, 0)),
            squares,
        ],
        out_specs=[lead(3, M, PAIR), pl.BlockSpec((dests, 1, 3 * M, PAIR), lambda p: (0, p, 0, 0))],
        out_shape=[shape((owned, 3, M, PAIR)), shape((dests, owned, 3 * M, PAIR), BF16)],
        compiler_params=params(),
    )(mix_all, comb_all, stat_all, inv)

    land_grads = pl.pallas_call(
        backward_kernel,
        grid=(owned,),
        in_specs=[lands, squares, steps, steps, steps, lead(3, M, PAIR)],
        out_specs=lead(2, M, PAIR),
        out_shape=shape((owned, 2, M, PAIR)),
        compiler_params=params(),
        cost_estimate=cost(24 * 12 * M**3 * 2 * owned, 8 * 2**20 * owned),
    )(land_own, soft, xs, ys, qs, full)

    got = spread_out(send[:, 0], spread, True) if shared else send[0]

    dq, dk, gv, part = pl.pallas_call(
        second_kernel,
        grid=(pairs,),
        in_specs=[cols] * 4 + [lands, lead(2 * M, rows), lead(2 * M, rows), lead(3 * M, PAIR)],
        out_specs=[cols, cols, cols, lands],
        out_shape=[shape((rows, width)), shape((rows, width)), shape((rows, width), BF16), shape((2, M, width))],
        compiler_params=params(),
    )(q, k, v, g, land, wf, eb, got)

    if shared:
        mine = lax.dynamic_slice_in_dim(part, me * PAIR, PAIR, 2) + land_grads[0]
        part = lax.dynamic_update_slice_in_dim(part, mine, me * PAIR, 2)
    else:
        extra = jnp.swapaxes(land_grads, 0, 1).transpose(0, 2, 1, 3).reshape(2, M, width)
        part = part + jnp.where(me == 0, 1.0, 0.0) * extra
    part = part.astype(BF16).reshape(2, spread, land_dev, width).swapaxes(0, 1)
    final = spread_out(part, spread, True)

    gq, gk = pl.pallas_call(
        functools.partial(last_kernel, spread),
        grid=(pairs,),
        in_specs=[cols, cols, pl.BlockSpec((spread, 2, land_dev, PAIR), lambda p: (0, 0, 0, p))],
        out_specs=[cols, cols],
        out_shape=[shape((rows, width), BF16)] * 2,
        compiler_params=params(),
    )(dq, dk, final)
    return gq[None], gk[None], gv[None]


def solution(mesh):
    spec = P(("groups", "batch"), "seq", "head")
    return jax.shard_map(per_device, mesh=mesh, in_specs=(spec,) * 4, out_specs=(spec,) * 3, check_vma=False)
```

```python
import functools
import math

import jax
import jax.numpy as jnp
from jax import lax
from jax.experimental import pallas as pl
from jax.experimental.pallas import tpu as pltpu
from jax.sharding import PartitionSpec as P

DH = 64
M = 256
ITERS = 4
PAIR = 2 * DH
TEMPER = DH ** (-0.5)
LOG2 = TEMPER * math.log2(math.e)
F32, BF16 = jnp.float32, jnp.bfloat16
HIGH = lax.Precision.HIGH
VMEM_LIMIT = 56 * 1024 * 1024


def mm(a, b, prec=None):
    return lax.dot_general(a, b, (((1,), (0,)), ((), ())), precision=prec, preferred_element_type=F32)


def nt(a, b, prec=None):
    return lax.dot_general(a, b, (((1,), (1,)), ((), ())), precision=prec, preferred_element_type=F32)


def tn(a, b, prec=None):
    return lax.dot_general(a, b, (((0,), (0,)), ((), ())), precision=prec, preferred_element_type=F32)


def own_half(shape, head):
    lane = lax.broadcasted_iota(jnp.int32, shape, len(shape) - 1)
    return lane < DH if head == 0 else lane >= DH


def only(x, head):
    return jnp.where(own_half(x.shape, head), x, jnp.zeros_like(x))


def stacked(x):
    return jnp.concatenate([only(x, 0), only(x, 1)], axis=0)


def halves(x):
    return jnp.where(own_half((M, PAIR), 0), x[:M], x[M:])


def landmark_kernel(q_ref, k_ref, out_ref):
    rows = q_ref.shape[0]
    land = out_ref.shape[1]
    seg = rows // land
    spot = lax.broadcasted_iota(jnp.int32, (land, rows), 0)
    place = lax.broadcasted_iota(jnp.int32, (land, rows), 1)
    member = jnp.where((place >= spot * seg) & (place < spot * seg + seg), 1.0, 0.0).astype(BF16)
    out_ref[0] = (mm(member, q_ref[...]) / seg).astype(BF16)
    out_ref[1] = (mm(member, k_ref[...]) / seg).astype(BF16)


def first_kernel(q_ref, k_ref, v_ref, g_ref, land_ref, wf_ref, eb_ref, mix_ref, comb_ref, stat_ref):
    lq, lk = stacked(land_ref[0]), stacked(land_ref[1])
    rows = q_ref.shape[0]
    for h in range(2):
        sf = nt(lk[h * M : (h + 1) * M], q_ref[...])
        top = jnp.max(sf, axis=0, keepdims=True)
        ef = jnp.exp2((sf - top) * LOG2)
        wf_ref[0, h * M : (h + 1) * M] = (ef * (1.0 / jnp.sum(ef, axis=0, keepdims=True))).astype(BF16)
    comb_ref[0] = halves(mm(wf_ref[0], g_ref[...])).astype(comb_ref.dtype)
    tops, mixes = [], []
    for h in range(2):
        sb = nt(lq[h * M : (h + 1) * M], k_ref[...])
        top = jnp.max(sb, axis=1, keepdims=True)
        eb = jnp.exp2((sb - top) * LOG2).astype(BF16)
        eb_ref[0, h * M : (h + 1) * M] = eb
        values = jnp.where(own_half((rows, PAIR), h), v_ref[...], jnp.ones_like(v_ref[...]))
        mixes.append(mm(eb, values))
        tops.append(jnp.broadcast_to(top, (M, PAIR)))
    low = own_half((M, PAIR), 0)
    mix_ref[0] = jnp.where(low, mixes[0], mixes[1]).astype(mix_ref.dtype)
    total = jnp.where(low, mixes[1], mixes[0])
    tall = jnp.where(low, tops[1], tops[0])
    tall_t, total_t = tall.T, total.T
    stat_ref[0] = jnp.concatenate(
        [tall_t[DH : DH + 1], tall_t[0:1], total_t[DH : DH + 1], total_t[0:1], jnp.zeros((4, M), F32)], axis=0
    )


def forward_kernel(land_ref, soft_ref, x_ref, y_ref, q_ref, inv_ref):
    lq, lk = land_ref[0], land_ref[1]
    rowi = lax.broadcasted_iota(jnp.int32, (M, M), 0)
    coli = lax.broadcasted_iota(jnp.int32, (M, M), 1)
    eye = jnp.where(rowi == coli, 1.0, 0.0)
    soft, scale, xs, prods = [], [], [], []
    for h in range(2):
        s = nt(only(lq, h), lk)
        e = jnp.exp2((s - jnp.max(s, axis=1, keepdims=True)) * LOG2)
        a = e / jnp.sum(e, axis=1, keepdims=True)
        soft_ref[0, h] = a
        inv_s = 1.0 / (jnp.max(jnp.sum(a, axis=0, keepdims=True), axis=1, keepdims=True)
                       * jnp.max(jnp.sum(a, axis=1, keepdims=True), axis=0, keepdims=True))
        soft.append(a)
        scale.append(inv_s)
        xs.append(nt(a, a, HIGH) * inv_s)
        prods.append(None)
    for k in range(ITERS):
        ys = [mm(x, x, HIGH) for x in xs]
        ts = [mm(x, y, HIGH) for x, y in zip(xs, ys)]
        for h in range(2):
            x_ref[0, h, k] = xs[h]
            y_ref[0, h, k] = ys[h]
            q = 3.25 * eye - 3.75 * xs[h] + 1.75 * ys[h] - 0.25 * ts[h]
            q_ref[0, h, k] = q
            prods[h] = q if k == 0 else mm(prods[h], q, HIGH)
            if k < ITERS - 1:
                xs[h] = mm(xs[h], q, HIGH)
    for h in range(2):
        inv_ref[0, h] = tn(soft[h], prods[h], HIGH) * scale[h]


def middle(parts, dests, mixes, combs, stats_in, inv_ref, full_ref, send, send_stat):
    stats = []
    for d in range(parts):
        st = stats_in[d]
        def column(r0, r1):
            wide = jnp.concatenate([jnp.broadcast_to(st[r0 : r0 + 1], (DH, M)), jnp.broadcast_to(st[r1 : r1 + 1], (DH, M))], axis=0)
            return wide.T
        stats.append((column(0, 1), column(2, 3)))
    top = functools.reduce(jnp.maximum, [s[0] for s in stats])
    shrink = [jnp.exp2((s[0] - top) * LOG2) for s in stats]
    total = sum(f * s[1] for f, s in zip(shrink, stats))
    inv_total = 1.0 / total
    mixed = sum(f * mixes[d].astype(F32) for d, f in enumerate(shrink)) * inv_total
    gcomb = sum(combs[d].astype(F32) for d in range(parts))
    full_ref[0, 0] = mixed
    full_ref[0, 1] = gcomb
    comb, gm = [], []
    for h in range(2):
        comb.append(mm(inv_ref[0, h], only(mixed, h), HIGH))
        gm.append(tn(inv_ref[0, h], only(gcomb, h), HIGH))
    combined = comb[0] + comb[1]
    gmix = gm[0] + gm[1]
    full_ref[0, 2] = combined
    for i in range(dests):
        if dests == parts:
            factor = shrink[i] * inv_total
        else:
            me = lax.axis_index("seq")
            factor = sum(jnp.where(me == d, shrink[d], 0.0) for d in range(parts)) * inv_total
        scaled = (gmix * factor).astype(BF16)
        dot = scaled.astype(F32) * mixed
        rd = [-jnp.sum(only(dot, h), axis=1, keepdims=True) for h in range(2)]
        low = own_half((M, PAIR), 0)
        wide = jnp.where(low, jnp.broadcast_to(rd[0], (M, PAIR)), jnp.broadcast_to(rd[1], (M, PAIR))).T
        send(i, combined.astype(BF16), scaled)
        send_stat(i, jnp.concatenate([wide[0:1], wide[DH : DH + 1], jnp.zeros((6, M), F32)], axis=0))


def middle_kernel(parts, mix_ref, comb_ref, stat_ref, inv_ref, full_ref, send_ref, rd_ref):
    def send(i, combined, scaled):
        send_ref[0, :M] = combined
        send_ref[0, M:] = scaled

    def send_stat(i, rd):
        rd_ref[0] = rd

    each = range(parts)
    middle(parts, 1, [mix_ref[d, 0] for d in each], [comb_ref[d, 0] for d in each], [stat_ref[d, 0] for d in each], inv_ref, full_ref, send, send_stat)


def sym(x):
    return 0.5 * (x + x.T)


def backward_kernel(land_ref, soft_ref, x_ref, y_ref, q_ref, full_ref, out_ref):
    mixed, gcomb, combined = full_ref[0, 0], full_ref[0, 1], full_ref[0, 2]
    soft = [soft_ref[0, h] for h in range(2)]
    col = [jnp.sum(a, axis=0, keepdims=True) for a in soft]
    row = [jnp.sum(a, axis=1, keepdims=True) for a in soft]
    cn = [jnp.max(c, axis=1, keepdims=True) for c in col]
    rn = [jnp.max(r, axis=0, keepdims=True) for r in row]
    inv_s = [1.0 / (c * r) for c, r in zip(cn, rn)]
    gc = [only(gcomb, h) for h in range(2)]
    us = [[mm(soft[h], gc[h], HIGH) * inv_s[h]] for h in range(2)]
    ms = [[only(mixed, h)] for h in range(2)]
    for k in range(ITERS - 1):
        for h in range(2):
            us[h].append(mm(q_ref[0, h, k], us[h][-1], HIGH))
            ms[h].append(mm(q_ref[0, h, ITERS - 1 - k], ms[h][-1], HIGH))
    rm = [mm(q_ref[0, h, 0], ms[h][-1], HIGH) for h in range(2)]
    b = [None, None]
    for k in reversed(range(ITERS)):
        xs = [x_ref[0, h, k] for h in range(2)]
        ys = [y_ref[0, h, k] for h in range(2)]
        c = []
        for h in range(2):
            u, m = us[h][k], ms[h][ITERS - 1 - k]
            c.append(0.5 * nt(u + pltpu.roll(m, DH, 1), m + pltpu.roll(u, DH, 1), HIGH))
        t = [-0.25 * c[h] if b[h] is None else 1.75 * b[h] - 0.25 * c[h] for h in range(2)]
        tx = [mm(t[h], xs[h], HIGH) for h in range(2)]
        ty = [mm(t[h], ys[h], HIGH) for h in range(2)]
        for h in range(2):
            if b[h] is None:
                yb = 1.75 * c[h] + sym(tx[h])
                xb = -3.75 * c[h]
            else:
                by = mm(b[h], ys[h], HIGH)
                yb = 1.75 * c[h] - 3.75 * b[h] + sym(tx[h] - 0.5 * by)
                xb = 3.25 * b[h] - 3.75 * c[h]
            b[h] = xb + sym(ty[h] + 2.0 * mm(yb, xs[h], HIGH))
    lq, lk = land_ref[0].astype(F32), land_ref[1].astype(F32)
    qa, ka = [], []
    for h in range(2):
        a = soft[h]
        sbar = -inv_s[h] * (
            jnp.sum(jnp.sum(gc[h] * combined, axis=1, keepdims=True), axis=0, keepdims=True)
            + jnp.sum(jnp.sum(b[h] * x_ref[0, h, 0], axis=1, keepdims=True), axis=0, keepdims=True)
        )
        grad = inv_s[h] * (nt(rm[h], gc[h], HIGH) + 2.0 * mm(b[h], a, HIGH))
        atc = jnp.where(col[h] == cn[h], 1.0, 0.0)
        atr = jnp.where(row[h] == rn[h], 1.0, 0.0)
        grad += atc * (sbar * rn[h] / jnp.sum(atc, axis=1, keepdims=True))
        grad += atr * (sbar * cn[h] / jnp.sum(atr, axis=0, keepdims=True))
        dsa = a * (grad - jnp.sum(grad * a, axis=1, keepdims=True))
        qa.append(mm(dsa, lk, HIGH))
        ka.append(tn(dsa, lq, HIGH))
    low = own_half((M, PAIR), 0)
    out_ref[0, 0] = TEMPER * jnp.where(low, qa[0], qa[1])
    out_ref[0, 1] = TEMPER * jnp.where(low, ka[0], ka[1])


def second_kernel(q_ref, k_ref, v_ref, g_ref, land_ref, wf_ref, eb_ref, got_ref, rd_ref, dq_ref, dk_ref, gv_ref, part_ref):
    lq, lk = stacked(land_ref[0]), stacked(land_ref[1])
    rows = q_ref.shape[0]
    comb = stacked(got_ref[0, 0:M])
    dsf = []
    for h in range(2):
        gf = nt(comb[h * M : (h + 1) * M], g_ref[...])
        w = wf_ref[0, h * M : (h + 1) * M].astype(F32)
        r = jnp.sum(gf * w, axis=0, keepdims=True)
        dsf.append((w * (gf - r)).astype(BF16))
    dsf = jnp.concatenate(dsf, axis=0)
    dq_ref[...] = TEMPER * tn(lk, dsf).T
    part_ref[1] = TEMPER * halves(mm(dsf, q_ref[...]))
    dsb, gms = [], []
    for h in range(2):
        st = rd_ref[0]
        rd = jnp.broadcast_to(st[h : h + 1], (PAIR, M)).T
        hi = rd.astype(BF16)
        lo = (rd - hi.astype(F32)).astype(BF16)
        lane = lax.broadcasted_iota(jnp.int32, (M, PAIR), 1)
        start = DH if h == 0 else 0
        rest = jnp.where(lane == start, hi, jnp.where(lane == start + 1, lo, jnp.zeros_like(hi)))
        gx = jnp.where(own_half((M, PAIR), h), got_ref[0, M : 2 * M], rest)
        values = jnp.where(own_half((rows, PAIR), h), v_ref[...], jnp.ones_like(v_ref[...]))
        gb = nt(gx, values)
        dsb.append((eb_ref[0, h * M : (h + 1) * M].astype(F32) * gb).astype(BF16))
        gms.append(only(gx, h))
    dsb = jnp.concatenate(dsb, axis=0)
    gms = jnp.concatenate(gms, axis=0)
    gv_ref[...] = tn(gms, eb_ref[0]).T.astype(BF16)
    part_ref[0] = TEMPER * halves(mm(dsb, k_ref[...]))
    dk_ref[...] = TEMPER * tn(lq, dsb).T


def last_kernel(parts, dq_ref, dk_ref, got_ref, gq_ref, gk_ref):
    land = got_ref.shape[2]
    rows = dq_ref.shape[0]
    seg = rows // land
    for i, (src, dst) in enumerate(((dq_ref, gq_ref), (dk_ref, gk_ref))):
        total = sum(got_ref[d, i].astype(F32) for d in range(parts)) / seg
        wide = jnp.broadcast_to(total[:, None, :], (land, seg, PAIR)).reshape(rows, PAIR)
        dst[...] = (src[...] + wide).astype(BF16)


def params():
    return pltpu.CompilerParams(vmem_limit_bytes=VMEM_LIMIT)


def cost(flops, moved):
    return pl.CostEstimate(flops=int(flops), bytes_accessed=int(moved), transcendentals=0)


def shape(dims, dtype=F32):
    return jax.ShapeDtypeStruct(dims, dtype)


def spread_out(x, spread, personal):
    me = lax.axis_index("seq")
    def to(d):
        return lax.dynamic_index_in_dim(x, d, 0, keepdims=False) if personal else x
    got = [to(me)]
    for step in range(1, spread):
        perm = [(i, (i + step) % spread) for i in range(spread)]
        got.append(lax.ppermute(to(lax.rem(me + step, spread)), "seq", perm))
    table = jnp.stack(got)
    return jnp.stack([lax.dynamic_index_in_dim(table, lax.rem(me - s + spread, spread), 0, keepdims=False) for s in range(spread)])


def general(q, k, v, g):
    rows, width = q.shape
    spread = lax.axis_size("seq")
    me = lax.axis_index("seq")
    land_dev = M // spread
    pairs = width // PAIR
    owned = pairs

    land = pl.pallas_call(landmark_kernel, out_shape=shape((2, land_dev, width), BF16), compiler_params=params())(q, k)
    land = spread_out(land, spread, False)
    land = jnp.swapaxes(land, 0, 1).reshape(2, M, width)

    cols = pl.BlockSpec((rows, PAIR), lambda p: (0, p))
    lands = pl.BlockSpec((2, M, PAIR), lambda p: (0, 0, p))
    def lead(*dims):
        return pl.BlockSpec((1,) + dims, lambda p: (p,) + (0,) * len(dims))
    wf, eb, mix, comb, stat = pl.pallas_call(
        first_kernel,
        grid=(pairs,),
        in_specs=[cols] * 4 + [lands],
        out_specs=[lead(2 * M, rows), lead(2 * M, rows), lead(M, PAIR), lead(M, PAIR), lead(8, M)],
        out_shape=[shape((pairs, 2 * M, rows), BF16), shape((pairs, 2 * M, rows), BF16), shape((pairs, M, PAIR)), shape((pairs, M, PAIR)), shape((pairs, 8, M))],
        compiler_params=params(),
    )(q, k, v, g, land)

    land_own = land
    squares = lead(2, M, M)
    steps = lead(2, ITERS, M, M)
    soft, xs, ys, qs, inv = pl.pallas_call(
        forward_kernel,
        grid=(owned,),
        in_specs=[lands],
        out_specs=[squares, steps, steps, steps, squares],
        out_shape=[shape((owned, 2, M, M))] + [shape((owned, 2, ITERS, M, M))] * 3 + [shape((owned, 2, M, M))],
        compiler_params=params(),
        cost_estimate=cost(16 * 12 * M**3 * 2 * owned, 8 * 2**20 * owned),
    )(land_own)

    mix_all, comb_all, stat_all = (lax.all_gather(x, "seq") for x in (mix, comb, stat))
    full, got, rd = pl.pallas_call(
        functools.partial(middle_kernel, spread),
        grid=(owned,),
        in_specs=[
            pl.BlockSpec((spread, 1, M, PAIR), lambda p: (0, p, 0, 0)),
            pl.BlockSpec((spread, 1, M, PAIR), lambda p: (0, p, 0, 0)),
            pl.BlockSpec((spread, 1, 8, M), lambda p: (0, p, 0, 0)),
            squares,
        ],
        out_specs=[lead(3, M, PAIR), lead(2 * M, PAIR), lead(8, M)],
        out_shape=[shape((owned, 3, M, PAIR)), shape((owned, 2 * M, PAIR), BF16), shape((owned, 8, M))],
        compiler_params=params(),
    )(mix_all, comb_all, stat_all, inv)

    land_grads = pl.pallas_call(
        backward_kernel,
        grid=(owned,),
        in_specs=[lands, squares, steps, steps, steps, lead(3, M, PAIR)],
        out_specs=lead(2, M, PAIR),
        out_shape=shape((owned, 2, M, PAIR)),
        compiler_params=params(),
        cost_estimate=cost(24 * 12 * M**3 * 2 * owned, 8 * 2**20 * owned),
    )(land_own, soft, xs, ys, qs, full)

    dq, dk, gv, part = pl.pallas_call(
        second_kernel,
        grid=(pairs,),
        in_specs=[cols] * 4 + [lands, lead(2 * M, rows), lead(2 * M, rows), lead(2 * M, PAIR), lead(8, M)],
        out_specs=[cols, cols, cols, lands],
        out_shape=[shape((rows, width)), shape((rows, width)), shape((rows, width), BF16), shape((2, M, width))],
        compiler_params=params(),
    )(q, k, v, g, land, wf, eb, got, rd)

    extra = jnp.swapaxes(land_grads, 0, 1).transpose(0, 2, 1, 3).reshape(2, M, width)
    part = part + jnp.where(me == 0, 1.0, 0.0) * extra
    part = part.astype(BF16).reshape(2, spread, land_dev, width).swapaxes(0, 1)
    final = spread_out(part, spread, True)

    gq, gk = pl.pallas_call(
        functools.partial(last_kernel, spread),
        grid=(pairs,),
        in_specs=[cols, cols, pl.BlockSpec((spread, 2, land_dev, PAIR), lambda p: (0, 0, 0, p))],
        out_specs=[cols, cols],
        out_shape=[shape((rows, width), BF16)] * 2,
        compiler_params=params(),
    )(dq, dk, final)
    return gq, gk, gv


def whole_kernel(
    spread, q_ref, k_ref, v_ref, g_ref, gq_ref, gk_ref, gv_ref,
    own_land, land, wf, eb, bsend, ssend, brecv, srecv, soft, xs, ys, qs, inv, full, back, rback, got, rgot,
    extra, dq, dk, part, psend, fbuf,
    land_s, land_r, b_s, b_r, s_s, s_r, g_s, g_r, r_s, r_r, f_s, f_r,
):
    S = spread
    me = lax.axis_index("seq")
    others = range(1, S)
    land_dev = M // S

    def shift(n):
        return lax.rem(me + n, S)

    def lanes(p):
        return pl.ds(pl.multiple_of(p * PAIR, PAIR), PAIR)

    def remote(src, dst, send_sem, recv_sem, to):
        return pltpu.make_async_remote_copy(
            src_ref=src, dst_ref=dst, send_sem=send_sem, recv_sem=recv_sem,
            device_id={"seq": to}, device_id_type=pl.DeviceIdType.MESH,
        )

    barrier = pltpu.get_barrier_semaphore()
    for s in others:
        pl.semaphore_signal(barrier, inc=1, device_id={"seq": shift(s)}, device_id_type=pl.DeviceIdType.MESH)

    landmark_kernel(q_ref, k_ref, own_land)
    for p in range(S):
        for i in range(2):
            land[p, me, i] = own_land[i, :, p * PAIR : (p + 1) * PAIR]
    pl.semaphore_wait(barrier, S - 1)

    def land_copy(i, s):
        p = shift(s + 1 + i)
        return remote(land.at[p, me], land.at[p, me], land_s.at[i, s - 1], land_r.at[i, s - 1], shift(s))

    for i in range(S):
        for s in others:
            land_copy(i, s).start()

    def lands(p):
        both = land[p]
        return both[:, 0].reshape(M, PAIR), both[:, 1].reshape(M, PAIR)

    def bundle_copy(i):
        return remote(bsend.at[i], brecv.at[i], b_s.at[i], b_r.at[i], shift(i + 1))

    def stat_copy(i):
        return remote(ssend.at[i], srecv.at[i], s_s.at[i], s_r.at[i], shift(i + 1))

    def first(i, carry):
        for s in others:
            land_copy(i, s).wait_recv()
        p = shift(i + 1)
        cols = lanes(p)
        first_kernel(
            q_ref.at[:, cols], k_ref.at[:, cols], v_ref.at[:, cols], g_ref.at[:, cols], lands(p),
            wf.at[pl.ds(p, 1)], eb.at[pl.ds(p, 1)],
            bsend.at[pl.ds(i, 1), 0:M], bsend.at[pl.ds(i, 1), M : 2 * M], ssend.at[pl.ds(i, 1)],
        )

        @pl.when(i < S - 1)
        def _():
            bundle_copy(i).start()
            stat_copy(i).start()

        return carry

    lax.fori_loop(0, S, first, 0)
    land_own = lands(me)
    forward_kernel(land_own, soft, xs, ys, qs, inv)
    for i in range(S - 1):
        bundle_copy(i).wait_recv()
        stat_copy(i).wait_recv()

    mixes = [bsend[S - 1, 0:M]] + [brecv[i, 0:M] for i in range(S - 1)]
    combs = [bsend[S - 1, M : 2 * M]] + [brecv[i, M : 2 * M] for i in range(S - 1)]
    stats = [ssend[S - 1]] + [srecv[i] for i in range(S - 1)]

    def back_copy(s):
        return remote(back.at[s - 1], got.at[me], g_s.at[s - 1], g_r.at[s - 1], shift(S - s))

    def rback_copy(s):
        return remote(rback.at[s - 1], rgot.at[me], r_s.at[s - 1], r_r.at[s - 1], shift(S - s))

    def send(s, combined, scaled):
        if s == 0:
            got[me, 0:M] = combined
            got[me, M : 2 * M] = scaled
        else:
            back[s - 1, 0:M] = combined
            back[s - 1, M : 2 * M] = scaled
            back_copy(s).start()

    def send_stat(s, rd):
        if s == 0:
            rgot[me] = rd
        else:
            rback[s - 1] = rd
            rback_copy(s).start()

    middle(S, S, mixes, combs, stats, inv, full, send, send_stat)
    backward_kernel(land_own, soft, xs, ys, qs, full, extra)
    for s in others:
        back_copy(s).wait_recv()
        rback_copy(s).wait_recv()

    def final_copy(p, s):
        return remote(psend.at[p, shift(s)], fbuf.at[s - 1, p], f_s.at[p, s - 1], f_r.at[p, s - 1], shift(s))

    def second(p, carry):
        cols = lanes(p)
        second_kernel(
            q_ref.at[:, cols], k_ref.at[:, cols], v_ref.at[:, cols], g_ref.at[:, cols], lands(p),
            wf.at[pl.ds(p, 1)], eb.at[pl.ds(p, 1)], got.at[pl.ds(p, 1)], rgot.at[pl.ds(p, 1)],
            dq.at[:, cols], dk.at[:, cols], gv_ref.at[:, cols], part,
        )
        share = jnp.where(p == me, 1.0, 0.0)
        for i in range(2):
            sums = (part[i] + share * extra[0, i]).astype(BF16)
            for d in range(S):
                psend[p, d, i] = sums[d * land_dev : (d + 1) * land_dev]
        for s in others:
            final_copy(p, s).start()
        return carry

    lax.fori_loop(0, S, second, 0)

    def last(p, carry):
        for s in others:
            final_copy(p, s).wait_recv()
        cols = lanes(p)
        rows = dq.shape[0]
        seg = rows // land_dev
        for i, (src, dst) in enumerate(((dq, gq_ref), (dk, gk_ref))):
            total = (psend[p, me, i].astype(F32) + sum(fbuf[s - 1, p, i].astype(F32) for s in others)) / seg
            wide = jnp.broadcast_to(total[:, None, :], (land_dev, seg, PAIR)).reshape(rows, PAIR)
            dst[:, cols] = (src[:, cols] + wide).astype(BF16)
        return carry

    lax.fori_loop(0, S, last, 0)

    for i in range(S):
        for s in others:
            land_copy(i, s).wait_send()
            final_copy(i, s).wait_send()
    for s in others:
        bundle_copy(s - 1).wait_send()
        stat_copy(s - 1).wait_send()
        back_copy(s).wait_send()
        rback_copy(s).wait_send()


def fused(q, k, v, g):
    rows, width = q.shape
    S = lax.axis_size("seq")
    land_dev = M // S
    V, sem = pltpu.VMEM, pltpu.SemaphoreType.DMA
    vm = pl.BlockSpec(memory_space=pltpu.VMEM)
    return pl.pallas_call(
        functools.partial(whole_kernel, S),
        out_shape=[shape((rows, width), BF16)] * 3,
        in_specs=[vm] * 4,
        out_specs=[vm] * 3,
        scratch_shapes=[
            V((2, land_dev, width), BF16),
            V((S, S, 2, land_dev, PAIR), BF16),
            V((S, 2 * M, rows), BF16),
            V((S, 2 * M, rows), BF16),
            V((S, 2 * M, PAIR), BF16),
            V((S, 8, M), F32),
            V((S - 1, 2 * M, PAIR), BF16),
            V((S - 1, 8, M), F32),
            V((1, 2, M, M), F32),
            V((1, 2, ITERS, M, M), F32),
            V((1, 2, ITERS, M, M), F32),
            V((1, 2, ITERS, M, M), F32),
            V((1, 2, M, M), F32),
            V((1, 3, M, PAIR), F32),
            V((S - 1, 2 * M, PAIR), BF16),
            V((S - 1, 8, M), F32),
            V((S, 2 * M, PAIR), BF16),
            V((S, 8, M), F32),
            V((1, 2, M, PAIR), F32),
            V((rows, width), F32),
            V((rows, width), F32),
            V((2, M, PAIR), F32),
            V((S, S, 2, land_dev, PAIR), BF16),
            V((S - 1, S, 2, land_dev, PAIR), BF16),
            sem((S, S - 1)), sem((S, S - 1)),
            sem((S - 1,)), sem((S - 1,)), sem((S - 1,)), sem((S - 1,)),
            sem((S - 1,)), sem((S - 1,)), sem((S - 1,)), sem((S - 1,)),
            sem((S, S - 1)), sem((S, S - 1)),
        ],
        compiler_params=pltpu.CompilerParams(vmem_limit_bytes=VMEM_LIMIT, collective_id=0, has_side_effects=True),
        cost_estimate=cost(2**34, 7 * 2**20),
    )(q, k, v, g)


def per_device(query_rows, key_rows, value_rows, grad_output):
    data = [x[0] for x in (query_rows, key_rows, value_rows, grad_output)]
    shared = data[0].shape[1] // PAIR == lax.axis_size("seq")
    return tuple(x[None] for x in (fused if shared else general)(*data))


def solution(mesh):
    spec = P(("groups", "batch"), "seq", "head")
    return jax.shard_map(per_device, mesh=mesh, in_specs=(spec,) * 4, out_specs=(spec,) * 3, check_vma=False)
```

```python
import functools
import math

import jax
import jax.numpy as jnp
from jax import lax
from jax.experimental import pallas as pl
from jax.experimental.pallas import tpu as pltpu
from jax.sharding import PartitionSpec as P

DH = 64
M = 256
ITERS = 4
PAIR = 2 * DH
TEMPER = DH ** (-0.5)
LOG2 = TEMPER * math.log2(math.e)
F32, BF16 = jnp.float32, jnp.bfloat16
HIGH = True
VMEM_LIMIT = 56 * 1024 * 1024


def dot(dims, a, b, exact):
    def one(x, y):
        return lax.dot_general(x, y, (dims, ((), ())), preferred_element_type=F32)

    if not exact:
        return one(a, b)
    ah, bh = a.astype(BF16), b.astype(BF16)
    al, bl = (a - ah.astype(F32)).astype(BF16), (b - bh.astype(F32)).astype(BF16)
    return one(ah, bh) + (one(al, bh) + one(ah, bl))


def mm(a, b, exact=False):
    return dot(((1,), (0,)), a, b, exact)


def nt(a, b, exact=False):
    return dot(((1,), (1,)), a, b, exact)


def tn(a, b, exact=False):
    return dot(((0,), (0,)), a, b, exact)


def own_half(shape, head):
    lane = lax.broadcasted_iota(jnp.int32, shape, len(shape) - 1)
    return lane < DH if head == 0 else lane >= DH


def only(x, head):
    return jnp.where(own_half(x.shape, head), x, jnp.zeros_like(x))


def stacked(x):
    return jnp.concatenate([only(x, 0), only(x, 1)], axis=0)


def halves(x):
    return jnp.where(own_half((M, PAIR), 0), x[:M], x[M:])


def landmark_kernel(q_ref, k_ref, out_ref):
    rows = q_ref.shape[0]
    land = out_ref.shape[1]
    seg = rows // land
    spot = lax.broadcasted_iota(jnp.int32, (land, rows), 0)
    place = lax.broadcasted_iota(jnp.int32, (land, rows), 1)
    member = jnp.where((place >= spot * seg) & (place < spot * seg + seg), 1.0, 0.0).astype(BF16)
    out_ref[0] = (mm(member, q_ref[...]) / seg).astype(BF16)
    out_ref[1] = (mm(member, k_ref[...]) / seg).astype(BF16)


def first_kernel(q_ref, k_ref, v_ref, g_ref, land_ref, wf_ref, eb_ref, mix_ref, comb_ref, stat_ref):
    lq, lk = stacked(land_ref[0]), stacked(land_ref[1])
    rows = q_ref.shape[0]
    for h in range(2):
        sf = nt(lk[h * M : (h + 1) * M], q_ref[...])
        top = jnp.max(sf, axis=0, keepdims=True)
        ef = jnp.exp2((sf - top) * LOG2)
        wf_ref[0, h * M : (h + 1) * M] = (ef * (1.0 / jnp.sum(ef, axis=0, keepdims=True))).astype(BF16)
    comb_ref[0] = halves(mm(wf_ref[0], g_ref[...])).astype(comb_ref.dtype)
    tops, mixes = [], []
    for h in range(2):
        sb = nt(lq[h * M : (h + 1) * M], k_ref[...])
        top = jnp.max(sb, axis=1, keepdims=True)
        eb = jnp.exp2((sb - top) * LOG2).astype(BF16)
        eb_ref[0, h * M : (h + 1) * M] = eb
        values = jnp.where(own_half((rows, PAIR), h), v_ref[...], jnp.ones_like(v_ref[...]))
        mixes.append(mm(eb, values))
        tops.append(jnp.broadcast_to(top, (M, PAIR)))
    low = own_half((M, PAIR), 0)
    mix_ref[0] = jnp.where(low, mixes[0], mixes[1]).astype(mix_ref.dtype)
    total = jnp.where(low, mixes[1], mixes[0])
    tall = jnp.where(low, tops[1], tops[0])
    tall_t, total_t = tall.T, total.T
    stat_ref[0] = jnp.concatenate(
        [tall_t[DH : DH + 1], tall_t[0:1], total_t[DH : DH + 1], total_t[0:1], jnp.zeros((4, M), F32)], axis=0
    )


def forward_kernel(land_ref, soft_ref, x_ref, y_ref, q_ref, inv_ref):
    lq, lk = land_ref[0], land_ref[1]
    rowi = lax.broadcasted_iota(jnp.int32, (M, M), 0)
    coli = lax.broadcasted_iota(jnp.int32, (M, M), 1)
    eye = jnp.where(rowi == coli, 1.0, 0.0)
    soft, scale, xs, prods = [], [], [], []
    for h in range(2):
        s = nt(only(lq, h), lk)
        e = jnp.exp2((s - jnp.max(s, axis=1, keepdims=True)) * LOG2)
        a = e / jnp.sum(e, axis=1, keepdims=True)
        soft_ref[0, h] = a
        inv_s = 1.0 / (jnp.max(jnp.sum(a, axis=0, keepdims=True), axis=1, keepdims=True)
                       * jnp.max(jnp.sum(a, axis=1, keepdims=True), axis=0, keepdims=True))
        soft.append(a)
        scale.append(inv_s)
        xs.append(nt(a, a, HIGH) * inv_s)
        prods.append(None)
    for k in range(ITERS):
        ys = [mm(x, x, HIGH) for x in xs]
        ts = [mm(x, y, HIGH) for x, y in zip(xs, ys)]
        for h in range(2):
            x_ref[0, h, k] = xs[h]
            y_ref[0, h, k] = ys[h]
            q = 3.25 * eye - 3.75 * xs[h] + 1.75 * ys[h] - 0.25 * ts[h]
            q_ref[0, h, k] = q
            prods[h] = q if k == 0 else mm(prods[h], q, HIGH)
            if k < ITERS - 1:
                xs[h] = mm(xs[h], q, HIGH)
    for h in range(2):
        inv_ref[0, h] = tn(soft[h], prods[h], HIGH) * scale[h]


def middle(parts, dests, mixes, combs, stats_in, inv_ref, full_ref, send, send_stat):
    stats = []
    for d in range(parts):
        st = stats_in[d]
        def column(r0, r1):
            wide = jnp.concatenate([jnp.broadcast_to(st[r0 : r0 + 1], (DH, M)), jnp.broadcast_to(st[r1 : r1 + 1], (DH, M))], axis=0)
            return wide.T
        stats.append((column(0, 1), column(2, 3)))
    top = functools.reduce(jnp.maximum, [s[0] for s in stats])
    shrink = [jnp.exp2((s[0] - top) * LOG2) for s in stats]
    total = sum(f * s[1] for f, s in zip(shrink, stats))
    inv_total = 1.0 / total
    mixed = sum(f * mixes[d].astype(F32) for d, f in enumerate(shrink)) * inv_total
    gcomb = sum(combs[d].astype(F32) for d in range(parts))
    full_ref[0, 0] = mixed
    full_ref[0, 1] = gcomb
    comb, gm = [], []
    for h in range(2):
        comb.append(mm(inv_ref[0, h], only(mixed, h), HIGH))
        gm.append(tn(inv_ref[0, h], only(gcomb, h), HIGH))
    combined = comb[0] + comb[1]
    gmix = gm[0] + gm[1]
    full_ref[0, 2] = combined
    for i in range(dests):
        if dests == parts:
            factor = shrink[i] * inv_total
        else:
            me = lax.axis_index("seq")
            factor = sum(jnp.where(me == d, shrink[d], 0.0) for d in range(parts)) * inv_total
        scaled = (gmix * factor).astype(BF16)
        dot = scaled.astype(F32) * mixed
        rd = [-jnp.sum(only(dot, h), axis=1, keepdims=True) for h in range(2)]
        low = own_half((M, PAIR), 0)
        wide = jnp.where(low, jnp.broadcast_to(rd[0], (M, PAIR)), jnp.broadcast_to(rd[1], (M, PAIR))).T
        send(i, combined.astype(BF16), scaled)
        send_stat(i, jnp.concatenate([wide[0:1], wide[DH : DH + 1], jnp.zeros((6, M), F32)], axis=0))


def middle_kernel(parts, mix_ref, comb_ref, stat_ref, inv_ref, full_ref, send_ref, rd_ref):
    def send(i, combined, scaled):
        send_ref[0, :M] = combined
        send_ref[0, M:] = scaled

    def send_stat(i, rd):
        rd_ref[0] = rd

    each = range(parts)
    middle(parts, 1, [mix_ref[d, 0] for d in each], [comb_ref[d, 0] for d in each], [stat_ref[d, 0] for d in each], inv_ref, full_ref, send, send_stat)


def sym(x):
    return 0.5 * (x + x.T)


def backward_kernel(land_ref, soft_ref, x_ref, y_ref, q_ref, full_ref, out_ref):
    mixed, gcomb, combined = full_ref[0, 0], full_ref[0, 1], full_ref[0, 2]
    soft = [soft_ref[0, h] for h in range(2)]
    col = [jnp.sum(a, axis=0, keepdims=True) for a in soft]
    row = [jnp.sum(a, axis=1, keepdims=True) for a in soft]
    cn = [jnp.max(c, axis=1, keepdims=True) for c in col]
    rn = [jnp.max(r, axis=0, keepdims=True) for r in row]
    inv_s = [1.0 / (c * r) for c, r in zip(cn, rn)]
    gc = [only(gcomb, h) for h in range(2)]
    us = [[mm(soft[h], gc[h], HIGH) * inv_s[h]] for h in range(2)]
    ms = [[only(mixed, h)] for h in range(2)]
    for k in range(ITERS - 1):
        for h in range(2):
            us[h].append(mm(q_ref[0, h, k], us[h][-1], HIGH))
            ms[h].append(mm(q_ref[0, h, ITERS - 1 - k], ms[h][-1], HIGH))
    rm = [mm(q_ref[0, h, 0], ms[h][-1], HIGH) for h in range(2)]
    b = [None, None]
    for k in reversed(range(ITERS)):
        xs = [x_ref[0, h, k] for h in range(2)]
        ys = [y_ref[0, h, k] for h in range(2)]
        c = []
        for h in range(2):
            u, m = us[h][k], ms[h][ITERS - 1 - k]
            c.append(0.5 * nt(u + pltpu.roll(m, DH, 1), m + pltpu.roll(u, DH, 1), HIGH))
        t = [-0.25 * c[h] if b[h] is None else 1.75 * b[h] - 0.25 * c[h] for h in range(2)]
        tx = [mm(t[h], xs[h], HIGH) for h in range(2)]
        ty = [mm(t[h], ys[h], HIGH) for h in range(2)]
        for h in range(2):
            if b[h] is None:
                yb = 1.75 * c[h] + sym(tx[h])
                xb = -3.75 * c[h]
            else:
                by = mm(b[h], ys[h], HIGH)
                yb = 1.75 * c[h] - 3.75 * b[h] + sym(tx[h] - 0.5 * by)
                xb = 3.25 * b[h] - 3.75 * c[h]
            b[h] = xb + sym(ty[h] + 2.0 * mm(yb, xs[h], HIGH))
    lq, lk = land_ref[0].astype(F32), land_ref[1].astype(F32)
    qa, ka = [], []
    for h in range(2):
        a = soft[h]
        sbar = -inv_s[h] * (
            jnp.sum(jnp.sum(gc[h] * combined, axis=1, keepdims=True), axis=0, keepdims=True)
            + jnp.sum(jnp.sum(b[h] * x_ref[0, h, 0], axis=1, keepdims=True), axis=0, keepdims=True)
        )
        grad = inv_s[h] * (nt(rm[h], gc[h], HIGH) + 2.0 * mm(b[h], a, HIGH))
        atc = jnp.where(col[h] == cn[h], 1.0, 0.0)
        atr = jnp.where(row[h] == rn[h], 1.0, 0.0)
        grad += atc * (sbar * rn[h] / jnp.sum(atc, axis=1, keepdims=True))
        grad += atr * (sbar * cn[h] / jnp.sum(atr, axis=0, keepdims=True))
        dsa = a * (grad - jnp.sum(grad * a, axis=1, keepdims=True))
        qa.append(mm(dsa, lk, HIGH))
        ka.append(tn(dsa, lq, HIGH))
    low = own_half((M, PAIR), 0)
    out_ref[0, 0] = TEMPER * jnp.where(low, qa[0], qa[1])
    out_ref[0, 1] = TEMPER * jnp.where(low, ka[0], ka[1])


def second_kernel(q_ref, k_ref, v_ref, g_ref, land_ref, wf_ref, eb_ref, got_ref, rd_ref, dq_ref, dk_ref, gv_ref, part_ref):
    lq, lk = stacked(land_ref[0]), stacked(land_ref[1])
    rows = q_ref.shape[0]
    comb = stacked(got_ref[0, 0:M])
    dsf = []
    for h in range(2):
        gf = nt(comb[h * M : (h + 1) * M], g_ref[...])
        w = wf_ref[0, h * M : (h + 1) * M].astype(F32)
        r = jnp.sum(gf * w, axis=0, keepdims=True)
        dsf.append((w * (gf - r)).astype(BF16))
    dsf = jnp.concatenate(dsf, axis=0)
    dq_ref[...] = TEMPER * tn(lk, dsf).T
    part_ref[1] = TEMPER * halves(mm(dsf, q_ref[...]))
    dsb, gms = [], []
    for h in range(2):
        st = rd_ref[0]
        rd = jnp.broadcast_to(st[h : h + 1], (PAIR, M)).T
        hi = rd.astype(BF16)
        lo = (rd - hi.astype(F32)).astype(BF16)
        lane = lax.broadcasted_iota(jnp.int32, (M, PAIR), 1)
        start = DH if h == 0 else 0
        rest = jnp.where(lane == start, hi, jnp.where(lane == start + 1, lo, jnp.zeros_like(hi)))
        gx = jnp.where(own_half((M, PAIR), h), got_ref[0, M : 2 * M], rest)
        values = jnp.where(own_half((rows, PAIR), h), v_ref[...], jnp.ones_like(v_ref[...]))
        gb = nt(gx, values)
        dsb.append((eb_ref[0, h * M : (h + 1) * M].astype(F32) * gb).astype(BF16))
        gms.append(only(gx, h))
    dsb = jnp.concatenate(dsb, axis=0)
    gms = jnp.concatenate(gms, axis=0)
    gv_ref[...] = tn(gms, eb_ref[0]).T.astype(BF16)
    part_ref[0] = TEMPER * halves(mm(dsb, k_ref[...]))
    dk_ref[...] = TEMPER * tn(lq, dsb).T


def last_kernel(parts, dq_ref, dk_ref, got_ref, gq_ref, gk_ref):
    land = got_ref.shape[2]
    rows = dq_ref.shape[0]
    seg = rows // land
    for i, (src, dst) in enumerate(((dq_ref, gq_ref), (dk_ref, gk_ref))):
        total = sum(got_ref[d, i].astype(F32) for d in range(parts)) / seg
        wide = jnp.broadcast_to(total[:, None, :], (land, seg, PAIR)).reshape(rows, PAIR)
        dst[...] = (src[...] + wide).astype(BF16)


def params():
    return pltpu.CompilerParams(vmem_limit_bytes=VMEM_LIMIT)


def cost(flops, moved):
    return pl.CostEstimate(flops=int(flops), bytes_accessed=int(moved), transcendentals=0)


def shape(dims, dtype=F32):
    return jax.ShapeDtypeStruct(dims, dtype)


def spread_out(x, spread, personal):
    me = lax.axis_index("seq")
    def to(d):
        return lax.dynamic_index_in_dim(x, d, 0, keepdims=False) if personal else x
    got = [to(me)]
    for step in range(1, spread):
        perm = [(i, (i + step) % spread) for i in range(spread)]
        got.append(lax.ppermute(to(lax.rem(me + step, spread)), "seq", perm))
    table = jnp.stack(got)
    return jnp.stack([lax.dynamic_index_in_dim(table, lax.rem(me - s + spread, spread), 0, keepdims=False) for s in range(spread)])


def general(q, k, v, g):
    rows, width = q.shape
    spread = lax.axis_size("seq")
    me = lax.axis_index("seq")
    land_dev = M // spread
    pairs = width // PAIR
    owned = pairs

    land = pl.pallas_call(landmark_kernel, out_shape=shape((2, land_dev, width), BF16), compiler_params=params())(q, k)
    land = spread_out(land, spread, False)
    land = jnp.swapaxes(land, 0, 1).reshape(2, M, width)

    cols = pl.BlockSpec((rows, PAIR), lambda p: (0, p))
    lands = pl.BlockSpec((2, M, PAIR), lambda p: (0, 0, p))
    def lead(*dims):
        return pl.BlockSpec((1,) + dims, lambda p: (p,) + (0,) * len(dims))
    wf, eb, mix, comb, stat = pl.pallas_call(
        first_kernel,
        grid=(pairs,),
        in_specs=[cols] * 4 + [lands],
        out_specs=[lead(2 * M, rows), lead(2 * M, rows), lead(M, PAIR), lead(M, PAIR), lead(8, M)],
        out_shape=[shape((pairs, 2 * M, rows), BF16), shape((pairs, 2 * M, rows), BF16), shape((pairs, M, PAIR)), shape((pairs, M, PAIR)), shape((pairs, 8, M))],
        compiler_params=params(),
    )(q, k, v, g, land)

    land_own = land
    squares = lead(2, M, M)
    steps = lead(2, ITERS, M, M)
    soft, xs, ys, qs, inv = pl.pallas_call(
        forward_kernel,
        grid=(owned,),
        in_specs=[lands],
        out_specs=[squares, steps, steps, steps, squares],
        out_shape=[shape((owned, 2, M, M))] + [shape((owned, 2, ITERS, M, M))] * 3 + [shape((owned, 2, M, M))],
        compiler_params=params(),
        cost_estimate=cost(16 * 12 * M**3 * 2 * owned, 8 * 2**20 * owned),
    )(land_own)

    mix_all, comb_all, stat_all = (lax.all_gather(x, "seq") for x in (mix, comb, stat))
    full, got, rd = pl.pallas_call(
        functools.partial(middle_kernel, spread),
        grid=(owned,),
        in_specs=[
            pl.BlockSpec((spread, 1, M, PAIR), lambda p: (0, p, 0, 0)),
            pl.BlockSpec((spread, 1, M, PAIR), lambda p: (0, p, 0, 0)),
            pl.BlockSpec((spread, 1, 8, M), lambda p: (0, p, 0, 0)),
            squares,
        ],
        out_specs=[lead(3, M, PAIR), lead(2 * M, PAIR), lead(8, M)],
        out_shape=[shape((owned, 3, M, PAIR)), shape((owned, 2 * M, PAIR), BF16), shape((owned, 8, M))],
        compiler_params=params(),
    )(mix_all, comb_all, stat_all, inv)

    land_grads = pl.pallas_call(
        backward_kernel,
        grid=(owned,),
        in_specs=[lands, squares, steps, steps, steps, lead(3, M, PAIR)],
        out_specs=lead(2, M, PAIR),
        out_shape=shape((owned, 2, M, PAIR)),
        compiler_params=params(),
        cost_estimate=cost(24 * 12 * M**3 * 2 * owned, 8 * 2**20 * owned),
    )(land_own, soft, xs, ys, qs, full)

    dq, dk, gv, part = pl.pallas_call(
        second_kernel,
        grid=(pairs,),
        in_specs=[cols] * 4 + [lands, lead(2 * M, rows), lead(2 * M, rows), lead(2 * M, PAIR), lead(8, M)],
        out_specs=[cols, cols, cols, lands],
        out_shape=[shape((rows, width)), shape((rows, width)), shape((rows, width), BF16), shape((2, M, width))],
        compiler_params=params(),
    )(q, k, v, g, land, wf, eb, got, rd)

    extra = jnp.swapaxes(land_grads, 0, 1).transpose(0, 2, 1, 3).reshape(2, M, width)
    part = part + jnp.where(me == 0, 1.0, 0.0) * extra
    part = part.astype(BF16).reshape(2, spread, land_dev, width).swapaxes(0, 1)
    final = spread_out(part, spread, True)

    gq, gk = pl.pallas_call(
        functools.partial(last_kernel, spread),
        grid=(pairs,),
        in_specs=[cols, cols, pl.BlockSpec((spread, 2, land_dev, PAIR), lambda p: (0, 0, 0, p))],
        out_specs=[cols, cols],
        out_shape=[shape((rows, width), BF16)] * 2,
        compiler_params=params(),
    )(dq, dk, final)
    return gq, gk, gv


def whole_kernel(
    spread, q_ref, k_ref, v_ref, g_ref, gq_ref, gk_ref, gv_ref,
    own_land, land, wf, eb, bsend, ssend, brecv, srecv, soft, xs, ys, qs, inv, full, back, rback, got, rgot,
    extra, dq, dk, part, psend, fbuf,
    land_s, land_r, b_s, b_r, s_s, s_r, g_s, g_r, r_s, r_r, f_s, f_r,
):
    S = spread
    me = lax.axis_index("seq")
    others = range(1, S)
    land_dev = M // S

    def shift(n):
        return lax.rem(me + n, S)

    def lanes(p):
        return pl.ds(pl.multiple_of(p * PAIR, PAIR), PAIR)

    def remote(src, dst, send_sem, recv_sem, to):
        return pltpu.make_async_remote_copy(
            src_ref=src, dst_ref=dst, send_sem=send_sem, recv_sem=recv_sem,
            device_id={"seq": to}, device_id_type=pl.DeviceIdType.MESH,
        )

    barrier = pltpu.get_barrier_semaphore()
    for s in others:
        pl.semaphore_signal(barrier, inc=1, device_id={"seq": shift(s)}, device_id_type=pl.DeviceIdType.MESH)

    landmark_kernel(q_ref, k_ref, own_land)
    for p in range(S):
        for i in range(2):
            land[p, me, i] = own_land[i, :, p * PAIR : (p + 1) * PAIR]
    pl.semaphore_wait(barrier, S - 1)

    def land_copy(i, s):
        p = shift(s + 1 + i)
        return remote(land.at[p, me], land.at[p, me], land_s.at[i, s - 1], land_r.at[i, s - 1], shift(s))

    for i in range(S):
        for s in others:
            land_copy(i, s).start()

    def lands(p):
        both = land[p]
        return both[:, 0].reshape(M, PAIR), both[:, 1].reshape(M, PAIR)

    def bundle_copy(i):
        return remote(bsend.at[i], brecv.at[i], b_s.at[i], b_r.at[i], shift(i + 1))

    def stat_copy(i):
        return remote(ssend.at[i], srecv.at[i], s_s.at[i], s_r.at[i], shift(i + 1))

    def first(i, carry):
        for s in others:
            land_copy(i, s).wait_recv()
        p = shift(i + 1)
        cols = lanes(p)
        first_kernel(
            q_ref.at[:, cols], k_ref.at[:, cols], v_ref.at[:, cols], g_ref.at[:, cols], lands(p),
            wf.at[pl.ds(p, 1)], eb.at[pl.ds(p, 1)],
            bsend.at[pl.ds(i, 1), 0:M], bsend.at[pl.ds(i, 1), M : 2 * M], ssend.at[pl.ds(i, 1)],
        )

        @pl.when(i < S - 1)
        def _():
            bundle_copy(i).start()
            stat_copy(i).start()

        return carry

    lax.fori_loop(0, S, first, 0)
    land_own = lands(me)
    forward_kernel(land_own, soft, xs, ys, qs, inv)
    for i in range(S - 1):
        bundle_copy(i).wait_recv()
        stat_copy(i).wait_recv()

    mixes = [bsend[S - 1, 0:M]] + [brecv[i, 0:M] for i in range(S - 1)]
    combs = [bsend[S - 1, M : 2 * M]] + [brecv[i, M : 2 * M] for i in range(S - 1)]
    stats = [ssend[S - 1]] + [srecv[i] for i in range(S - 1)]

    def back_copy(s):
        return remote(back.at[s - 1], got.at[me], g_s.at[s - 1], g_r.at[s - 1], shift(S - s))

    def rback_copy(s):
        return remote(rback.at[s - 1], rgot.at[me], r_s.at[s - 1], r_r.at[s - 1], shift(S - s))

    def send(s, combined, scaled):
        if s == 0:
            got[me, 0:M] = combined
            got[me, M : 2 * M] = scaled
        else:
            back[s - 1, 0:M] = combined
            back[s - 1, M : 2 * M] = scaled
            back_copy(s).start()

    def send_stat(s, rd):
        if s == 0:
            rgot[me] = rd
        else:
            rback[s - 1] = rd
            rback_copy(s).start()

    middle(S, S, mixes, combs, stats, inv, full, send, send_stat)
    backward_kernel(land_own, soft, xs, ys, qs, full, extra)
    for s in others:
        back_copy(s).wait_recv()
        rback_copy(s).wait_recv()

    def final_copy(p, s):
        return remote(psend.at[p, shift(s)], fbuf.at[s - 1, p], f_s.at[p, s - 1], f_r.at[p, s - 1], shift(s))

    def second(p, carry):
        cols = lanes(p)
        second_kernel(
            q_ref.at[:, cols], k_ref.at[:, cols], v_ref.at[:, cols], g_ref.at[:, cols], lands(p),
            wf.at[pl.ds(p, 1)], eb.at[pl.ds(p, 1)], got.at[pl.ds(p, 1)], rgot.at[pl.ds(p, 1)],
            dq.at[:, cols], dk.at[:, cols], gv_ref.at[:, cols], part,
        )
        share = jnp.where(p == me, 1.0, 0.0)
        for i in range(2):
            sums = (part[i] + share * extra[0, i]).astype(BF16)
            for d in range(S):
                psend[p, d, i] = sums[d * land_dev : (d + 1) * land_dev]
        for s in others:
            final_copy(p, s).start()
        return carry

    lax.fori_loop(0, S, second, 0)

    def last(p, carry):
        for s in others:
            final_copy(p, s).wait_recv()
        cols = lanes(p)
        rows = dq.shape[0]
        seg = rows // land_dev
        for i, (src, dst) in enumerate(((dq, gq_ref), (dk, gk_ref))):
            total = (psend[p, me, i].astype(F32) + sum(fbuf[s - 1, p, i].astype(F32) for s in others)) / seg
            wide = jnp.broadcast_to(total[:, None, :], (land_dev, seg, PAIR)).reshape(rows, PAIR)
            dst[:, cols] = (src[:, cols] + wide).astype(BF16)
        return carry

    lax.fori_loop(0, S, last, 0)

    for i in range(S):
        for s in others:
            land_copy(i, s).wait_send()
            final_copy(i, s).wait_send()
    for s in others:
        bundle_copy(s - 1).wait_send()
        stat_copy(s - 1).wait_send()
        back_copy(s).wait_send()
        rback_copy(s).wait_send()


def fused(q, k, v, g):
    rows, width = q.shape
    S = lax.axis_size("seq")
    land_dev = M // S
    V, sem = pltpu.VMEM, pltpu.SemaphoreType.DMA
    vm = pl.BlockSpec(memory_space=pltpu.VMEM)
    return pl.pallas_call(
        functools.partial(whole_kernel, S),
        out_shape=[shape((rows, width), BF16)] * 3,
        in_specs=[vm] * 4,
        out_specs=[vm] * 3,
        scratch_shapes=[
            V((2, land_dev, width), BF16),
            V((S, S, 2, land_dev, PAIR), BF16),
            V((S, 2 * M, rows), BF16),
            V((S, 2 * M, rows), BF16),
            V((S, 2 * M, PAIR), BF16),
            V((S, 8, M), F32),
            V((S - 1, 2 * M, PAIR), BF16),
            V((S - 1, 8, M), F32),
            V((1, 2, M, M), F32),
            V((1, 2, ITERS, M, M), F32),
            V((1, 2, ITERS, M, M), F32),
            V((1, 2, ITERS, M, M), F32),
            V((1, 2, M, M), F32),
            V((1, 3, M, PAIR), F32),
            V((S - 1, 2 * M, PAIR), BF16),
            V((S - 1, 8, M), F32),
            V((S, 2 * M, PAIR), BF16),
            V((S, 8, M), F32),
            V((1, 2, M, PAIR), F32),
            V((rows, width), F32),
            V((rows, width), F32),
            V((2, M, PAIR), F32),
            V((S, S, 2, land_dev, PAIR), BF16),
            V((S - 1, S, 2, land_dev, PAIR), BF16),
            sem((S, S - 1)), sem((S, S - 1)),
            sem((S - 1,)), sem((S - 1,)), sem((S - 1,)), sem((S - 1,)),
            sem((S - 1,)), sem((S - 1,)), sem((S - 1,)), sem((S - 1,)),
            sem((S, S - 1)), sem((S, S - 1)),
        ],
        compiler_params=pltpu.CompilerParams(vmem_limit_bytes=VMEM_LIMIT, collective_id=0, has_side_effects=True),
        cost_estimate=cost(2**34, 7 * 2**20),
    )(q, k, v, g)


def per_device(query_rows, key_rows, value_rows, grad_output):
    data = [x[0] for x in (query_rows, key_rows, value_rows, grad_output)]
    shared = data[0].shape[1] // PAIR == lax.axis_size("seq")
    return tuple(x[None] for x in (fused if shared else general)(*data))


def solution(mesh):
    spec = P(("groups", "batch"), "seq", "head")
    return jax.shard_map(per_device, mesh=mesh, in_specs=(spec,) * 4, out_specs=(spec,) * 3, check_vma=False)
```
